32 devices in a mesh: groups: 1, res: 16 (over z, y, core), chan: 2 (over x).
Axes of the slice: x: 2, y: 2, z: 4, core: 2. Of those that a mesh axis runs over, the one named last changes fastest.
Arguments:
- pair: bfloat16 [128, 256, 256], P(('groups', 'chan'), 'res'), may hold values from -6 to 6
- pair_mask: int32 [256, 256], P(('groups', 'res'), 'chan'), may hold values from 0 to 1, as said below
- norm_gain: float32 [128], replicated, may hold values from 0.1 to 1.9
- norm_bias: float32 [128], replicated, may hold values from -3 to 3
- w_edges: bfloat16 [128, 512], replicated, may hold values from -0.5 to 0.5
- w_gate: bfloat16 [128, 128], replicated, may hold values from -0.5 to 0.5
- out_gain: float32 [128], replicated, may hold values from 0.1 to 1.9
- out_bias: float32 [128], replicated, may hold values from -3 to 3
- w_out: bfloat16 [128, 128], replicated, may hold values from -0.5 to 0.5
Outputs:
- update: bfloat16 [128, 256, 256], P('groups', 'res', 'chan')
The draws below stay inside these ranges and needn't reach their ends.
Inputs may be any that keep to these rules, and one draw needn't show every extreme that they name: pair_mask[i, k] = v[i] v[k] for a token vector v that is 1 on a prefix of at least 128 tokens and 0 on the rest, with at least one token invalid.
All inputs are finite; a program needn't handle non-finite values.
Results may differ from the reference program's by a relative error of at most 0.0058.
Values may be sent and summed in bfloat16 or wider, within the bound.
A program may use at most 64 MiB of HBM per device.

```python
import jax
import jax.numpy as jnp
from jax import lax

C = 128
CH = 128
ROWS_DEV = 16
TOKENS = 256


def draw_pair_mask(key, part):
    key = jax.random.fold_in(key, 11)
    valid_count = jax.random.randint(key, (), TOKENS // 2, TOKENS)
    positions = jnp.arange(TOKENS, dtype=jnp.int32)
    valid = (positions < valid_count).astype(jnp.int32)
    return valid[:, None] * valid[None, :]


def shard_levels(key, dims, pieces, smallest, largest):
    def one(dim, shards_of):
        heights = jax.random.uniform(jax.random.fold_in(jax.random.fold_in(key, 6), dim), (shards_of,), jnp.float32, smallest / len(pieces), largest / len(pieces))
        return jnp.repeat(jnp.exp(heights), dims[dim] // shards_of).reshape((-1,) + (1,) * (len(dims) - dim - 1))

    level = one(*pieces[0])
    for cut in pieces[1:]:
        level = level * one(*cut)
    return level


def scatter_about(rng, extent, deviation, bound, shards=(), kind=jnp.bfloat16):
    drawn = deviation * jax.random.normal(rng, extent, jnp.float32)
    if shards:
        drawn = drawn * shard_levels(rng, extent, shards, -0.22, 0.18)
    return jnp.clip(drawn, -bound, bound).astype(kind)


def setup_inputs(seed: int = 0, part: int = 0) -> dict:
    keys = jax.random.split(jax.random.key(seed), 10)
    part_splits = jax.random.split(jax.random.fold_in(keys[9], part), 10)
    pair = scatter_about(part_splits[0], (C, TOKENS, TOKENS), 1.0, 6.0, ((0, 2), (1, 16)))
    pair_mask = draw_pair_mask(jax.random.fold_in(jax.random.fold_in(keys[9], part), 71), part)
    norm_gain = jnp.clip(1.0 + 0.18 * jax.random.normal(keys[2], (C,), jnp.float32), 0.1, 1.9)
    norm_bias = scatter_about(keys[3], (C,), 0.5, 3.0, (), jnp.float32)
    w_edges = scatter_about(keys[4], (C, 4 * CH), C ** -0.5, 0.5)
    w_gate = scatter_about(keys[5], (C, C), C ** -0.5, 0.5)
    out_gain = jnp.clip(1.0 + 0.18 * jax.random.normal(keys[6], (CH,), jnp.float32), 0.1, 1.9)
    out_bias = scatter_about(keys[7], (CH,), 0.5, 3.0, (), jnp.float32)
    w_out = scatter_about(keys[8], (CH, C), CH ** -0.5, 0.5)
    return {"pair": pair, "pair_mask": pair_mask, "norm_gain": norm_gain, "norm_bias": norm_bias, "w_edges": w_edges, "w_gate": w_gate, "out_gain": out_gain, "out_bias": out_bias, "w_out": w_out}


epsilon = 1e-05

def layer_norm(values, scale_gain, shift_bias):
    average = lax.optimization_barrier(jnp.mean(values, axis=0, keepdims=True))
    centered = values - average
    variance = lax.optimization_barrier(jnp.mean(centered * centered, axis=0, keepdims=True))
    return centered * lax.rsqrt(variance + epsilon) * scale_gain[:, None, None] + shift_bias[:, None, None]

def reference(pair, pair_mask, norm_gain, norm_bias, w_edges, w_gate, out_gain, out_bias, w_out):
    block_count = TOKENS // ROWS_DEV
    pair_blocks = pair.reshape(C, block_count, ROWS_DEV, TOKENS).transpose(1, 0, 2, 3)
    mask_blocks = pair_mask.reshape(block_count, ROWS_DEV, TOKENS)
    edge_weight = w_edges.astype(jnp.float32)

    def normalize(pair_block):
        return layer_norm(pair_block.astype(jnp.float32), norm_gain, norm_bias).astype(jnp.bfloat16)

    def edge_rows(inputs_pair):
        pair_block, mask_block = inputs_pair
        normed = normalize(pair_block).astype(jnp.float32)
        projected = jnp.einsum('cij,ch->hij', normed, edge_weight)
        maskf = mask_block.astype(jnp.float32)[None]
        left_edges = (jax.nn.sigmoid(projected[:CH]) * projected[CH:2 * CH] * maskf).astype(jnp.bfloat16)
        right_edges = (jax.nn.sigmoid(projected[2 * CH:3 * CH]) * projected[3 * CH:] * maskf).astype(jnp.bfloat16)
        return (left_edges, right_edges)
    left_blocks, right_blocks = lax.map(edge_rows, (pair_blocks, mask_blocks))
    left_edges = left_blocks.transpose(1, 0, 2, 3).reshape(CH, TOKENS, TOKENS)
    right_edges = right_blocks.transpose(1, 0, 2, 3).reshape(CH, TOKENS, TOKENS)

    def channel(inputs_pair):
        left_one, right_one = inputs_pair
        return jnp.dot(left_one.astype(jnp.float32), right_one.astype(jnp.float32).T, preferred_element_type=jnp.float32).astype(jnp.bfloat16)
    product = lax.map(channel, (left_edges, right_edges))
    product_blocks = product.reshape(CH, block_count, ROWS_DEV, TOKENS).transpose(1, 0, 2, 3)

    def finish(inputs_pair):
        pair_block, product_block = inputs_pair
        normed = normalize(pair_block).astype(jnp.float32)
        gate_values = jax.nn.sigmoid(jnp.einsum('cij,cd->dij', normed, w_gate.astype(jnp.float32)))
        product_normed = layer_norm(product_block.astype(jnp.float32), out_gain, out_bias).astype(jnp.bfloat16)
        mixed_out = jnp.einsum('hij,hd->dij', product_normed.astype(jnp.float32), w_out.astype(jnp.float32))
        return (gate_values * mixed_out).astype(jnp.bfloat16)
    update_blocks = lax.map(finish, (pair_blocks, product_blocks))
    return update_blocks.transpose(1, 0, 2, 3).reshape(C, TOKENS, TOKENS)
```

```python
import functools

import jax
import jax.numpy as jnp
from jax import lax
from jax.experimental import pallas as pl
from jax.experimental.pallas import tpu as pltpu
from jax.sharding import PartitionSpec as P

epsilon = 1e-05
MESH = pl.DeviceIdType.MESH
PLANE_ROWS = 4
CHUNKS = 4
VMEM_LIMIT = 48 * 1024 * 1024


def layer_norm(values, scale_gain, shift_bias):
    average = jnp.mean(values, axis=0, keepdims=True)
    centered = values - average
    variance = jnp.mean(centered * centered, axis=0, keepdims=True)
    return (
        centered * lax.rsqrt(variance + epsilon) * scale_gain[:, None, None]
        + shift_bias[:, None, None]
    )


def project_edges(normed, mask_block, w_edges):
    hidden = w_edges.shape[1] // 4
    maskf = mask_block.astype(jnp.float32)[None]

    def edge_half(offset):
        gate_part = jnp.einsum(
            "cij,ch->hij",
            normed,
            w_edges[:, offset : offset + hidden],
            preferred_element_type=jnp.float32,
        )
        value_part = jnp.einsum(
            "cij,ch->hij",
            normed,
            w_edges[:, offset + hidden : offset + 2 * hidden],
            preferred_element_type=jnp.float32,
        )
        return (jax.nn.sigmoid(gate_part) * value_part * maskf).astype(jnp.bfloat16)

    return (edge_half(0), edge_half(2 * hidden))


def finish(normed, product_normed, w_gate, w_out):
    gate_values = jax.nn.sigmoid(
        jnp.einsum("cij,cd->dij", normed, w_gate, preferred_element_type=jnp.float32)
    )
    mixed_out = jnp.einsum("hij,hd->dij", product_normed, w_out, preferred_element_type=jnp.float32)
    return (gate_values * mixed_out).astype(jnp.bfloat16)


def wide_body(pair, pair_mask, norm_gain, norm_bias, w_edges, w_gate, out_gain, out_bias, w_out):
    quarter = pair_mask.shape[1]
    whole_rows, mask_rows = (
        lax.all_gather(pair, "chan", axis=0, tiled=True),
        lax.all_gather(pair_mask, "chan", axis=1, tiled=True),
    )
    normed_rows = layer_norm(whole_rows.astype(jnp.float32), norm_gain, norm_bias).astype(
        jnp.bfloat16
    )
    left_edges, right_edges = project_edges(normed_rows, mask_rows, w_edges)
    left_edges, right_edges = (
        lax.all_to_all(left_edges, "res", split_axis=0, concat_axis=1, tiled=True),
        lax.all_to_all(right_edges, "res", split_axis=0, concat_axis=1, tiled=True),
    )
    right_slice = lax.dynamic_slice_in_dim(
        right_edges, lax.axis_index("chan") * quarter, quarter, 1
    )
    product = jnp.einsum(
        "cik,cjk->cij", left_edges, right_slice, preferred_element_type=jnp.float32
    )
    normed = lax.dynamic_slice_in_dim(normed_rows, lax.axis_index("chan") * quarter, quarter, 2)
    returned = lax.all_to_all(
        product.astype(jnp.bfloat16), "res", split_axis=1, concat_axis=0, tiled=True
    )
    product_normed = layer_norm(returned.astype(jnp.float32), out_gain, out_bias).astype(
        jnp.bfloat16
    )
    return finish(normed, product_normed, w_gate, w_out)


def norm_into(source_ref, gain_ref, bias_ref, target_ref):
    values = source_ref[...].astype(jnp.float32)
    average = jnp.mean(values, axis=0, keepdims=True)
    centered = values - average
    variance = jnp.mean(centered * centered, axis=0, keepdims=True)
    scaled = centered * lax.rsqrt(variance + epsilon)
    target_ref[...] = (scaled * gain_ref[...] + bias_ref[...]).astype(target_ref.dtype)


def exchange_kernel(pair_ref, gain_ref, bias_ref, normed_ref, whole, local_sem, send_sem, recv_sem):
    groups, res, x = lax.axis_index("groups"), lax.axis_index("res"), lax.axis_index("chan")
    other = 1 - x
    half, _, width = pair_ref.shape
    cols = width // 2
    barrier = pltpu.get_barrier_semaphore()
    pl.semaphore_signal(barrier, inc=1, device_id=(groups, res, other), device_id_type=MESH)
    pl.semaphore_wait(barrier, 1)
    place = whole.at[pl.ds(x * half, half)]
    copy = pltpu.make_async_remote_copy(
        src_ref=pair_ref.at[:, :, pl.ds(pl.multiple_of(other * cols, cols), cols)],
        dst_ref=place,
        send_sem=send_sem,
        recv_sem=recv_sem,
        device_id=(groups, res, other),
        device_id_type=MESH,
    )
    copy.start()
    local = pltpu.make_async_copy(
        pair_ref.at[:, :, pl.ds(pl.multiple_of(x * cols, cols), cols)], place, local_sem
    )
    local.start()
    local.wait()
    copy.wait()
    norm_into(whole, gain_ref, bias_ref, normed_ref)


def triangle_kernel(
    depth,
    left_ref,
    right_ref,
    gain_ref,
    bias_ref,
    out_ref,
    lefts,
    rights,
    products,
    returned,
    local_sem,
    right_send,
    right_recv,
    left_send,
    left_recv,
    up_send,
    up_recv,
    down_send,
    down_recv,
    back_send,
    back_recv,
):
    groups, res, x = lax.axis_index("groups"), lax.axis_index("res"), lax.axis_index("chan")
    z, r = res // PLANE_ROWS, res % PLANE_ROWS
    plane = 2 * PLANE_ROWS
    p = r * 2 + x
    rows, cols = left_ref.shape[1], left_ref.shape[2]
    mine = left_ref.shape[0] // plane
    step = mine // CHUNKS
    tall = PLANE_ROWS * rows

    def device(q):
        return (groups, z * PLANE_ROWS + q // 2, q % 2)

    def peer(offset):
        return (p + offset) % plane

    barrier = pltpu.get_barrier_semaphore()

    def greet(offset, carry):
        pl.semaphore_signal(barrier, inc=1, device_id=device(peer(offset)), device_id_type=MESH)
        return carry

    lax.fori_loop(1, plane, greet, 0)

    @pl.when(z < depth - 1)
    def _():
        pl.semaphore_signal(
            barrier, inc=1, device_id=(groups, res + PLANE_ROWS, x), device_id_type=MESH
        )

    @pl.when(z > 0)
    def _():
        pl.semaphore_signal(
            barrier, inc=1, device_id=(groups, res - PLANE_ROWS, x), device_id_type=MESH
        )

    beside = jnp.where(z < depth - 1, 1, 0) + jnp.where(z > 0, 1, 0)
    pl.semaphore_wait(barrier, plane - 1 + beside)

    here = pl.ds(pl.multiple_of(z * tall + r * rows, rows), rows)
    here_left = pl.ds(pl.multiple_of(r * rows, rows), rows)
    here_cols = pl.ds(pl.multiple_of(x * cols, cols), cols)

    def right_copy(offset, c):
        q = peer(offset)
        return pltpu.make_async_remote_copy(
            src_ref=right_ref.at[pl.ds(q * mine + c * step, step)],
            dst_ref=rights.at[pl.ds(c * step, step), here, here_cols],
            send_sem=right_send.at[offset, c],
            recv_sem=right_recv.at[offset, c],
            device_id=device(q),
            device_id_type=MESH,
        )

    def left_copy(offset):
        q = peer(offset)
        return pltpu.make_async_remote_copy(
            src_ref=left_ref.at[pl.ds(q * mine, mine)],
            dst_ref=lefts.at[:, here_left, here_cols],
            send_sem=left_send.at[offset],
            recv_sem=left_recv.at[offset],
            device_id=device(q),
            device_id_type=MESH,
        )

    own_right = pltpu.make_async_copy(
        right_ref.at[pl.ds(p * mine, mine)], rights.at[:, here, here_cols], local_sem.at[0]
    )
    own_left = pltpu.make_async_copy(
        left_ref.at[pl.ds(p * mine, mine)], lefts.at[:, here_left, here_cols], local_sem.at[1]
    )
    own_right.start()

    def over_peers(act):
        def one(offset, carry):
            act(offset)
            return carry

        lax.fori_loop(1, plane, one, 0)

    for c in range(CHUNKS):
        over_peers(lambda offset: right_copy(offset, c).start())
    own_left.start()
    over_peers(lambda offset: left_copy(offset).start())

    def hop(owner, c, upward, distance):
        block = rights.at[
            pl.ds(c * step, step), pl.ds(pl.multiple_of(owner * tall, tall), tall), :
        ]
        send, recv = (up_send, up_recv) if upward else (down_send, down_recv)
        return pltpu.make_async_remote_copy(
            src_ref=block,
            dst_ref=block,
            send_sem=send.at[distance, c],
            recv_sem=recv.at[distance, c],
            device_id=(groups, res + PLANE_ROWS if upward else res - PLANE_ROWS, x),
            device_id_type=MESH,
        )

    own_right.wait()
    for c in range(CHUNKS):
        over_peers(lambda offset: right_copy(offset, c).wait_recv())

        @pl.when(z < depth - 1)
        def _():
            hop(z, c, True, 0).start()

        @pl.when(z > 0)
        def _():
            hop(z, c, False, 0).start()

    def pass_on(distance, c):
        @pl.when(z >= distance)
        def _():
            hop(z - distance, c, True, distance - 1).wait_recv()

        @pl.when((z >= distance) & (z < depth - 1))
        def _():
            hop(z - distance, c, True, distance).start()

        @pl.when(z + distance < depth)
        def _():
            hop(z + distance, c, False, distance - 1).wait_recv()

        @pl.when((z + distance < depth) & (z > 0))
        def _():
            hop(z + distance, c, False, distance).start()

    near = z // (depth // 2)

    def back_copy(r_to, side, c):
        q = r_to * 2 + side
        offset = (q - p + plane) % plane
        return pltpu.make_async_remote_copy(
            src_ref=products.at[
                side, pl.ds(c * step, step), pl.ds(pl.multiple_of(r_to * rows, rows), rows), :
            ],
            dst_ref=returned.at[pl.ds(p * mine + c * step, step)],
            send_sem=back_send.at[offset, c],
            recv_sem=back_recv.at[offset, c],
            device_id=device(q),
            device_id_type=MESH,
        )

    def multiply(side, c):
        channels = pl.ds(c * step, step)
        result = lax.dot_general(
            lefts[channels],
            rights[channels, pl.ds(pl.multiple_of(side * cols, cols), cols), :],
            (((2,), (2,)), ((0,), (0,))),
            preferred_element_type=jnp.float32,
        )
        products[side, channels] = result.astype(products.dtype)

        def give(r_to, carry):
            @pl.when(r_to * 2 + side != p)
            def _():
                back_copy(r_to, side, c).start()

            return carry

        lax.fori_loop(0, PLANE_ROWS, give, 0)

    for c in range(CHUNKS):
        pass_on(1, c)
    own_left.wait()
    over_peers(lambda offset: left_copy(offset).wait_recv())
    for c in range(CHUNKS):
        multiply(near, c)
    for c in range(CHUNKS):
        for distance in range(2, depth):
            pass_on(distance, c)
        multiply(1 - near, c)

    own_back = pltpu.make_async_copy(
        products.at[x, :, here_left, :], returned.at[pl.ds(p * mine, mine)], local_sem.at[2]
    )
    own_back.start()
    own_back.wait()

    def back_wait(offset, c, receive):
        q = peer(offset)
        copy = back_copy(q // 2, q % 2, c)
        if receive:
            copy.wait_recv()
        else:
            copy.wait_send()

    for c in range(CHUNKS):
        over_peers(lambda offset: back_wait(offset, c, True))
    norm_into(returned, gain_ref, bias_ref, out_ref)

    for c in range(CHUNKS):
        over_peers(lambda offset: back_wait(offset, c, False))
        over_peers(lambda offset: right_copy(offset, c).wait_send())
        for distance in range(depth - 1):

            @pl.when((z >= distance) & (z < depth - 1))
            def _():
                hop(z - distance, c, True, distance).wait_send()

            @pl.when((z + distance < depth) & (z > 0))
            def _():
                hop(z + distance, c, False, distance).wait_send()

    over_peers(lambda offset: left_copy(offset).wait_send())


def vmem():
    return pl.BlockSpec(memory_space=pltpu.VMEM)


def plane_body(
    depth, pair, pair_mask, norm_gain, norm_bias, w_edges, w_gate, out_gain, out_bias, w_out
):
    rows, cols = pair_mask.shape
    channels, hidden = w_gate.shape[0], w_out.shape[0]
    width = 2 * cols
    plane = 2 * PLANE_ROWS
    mine = hidden // plane
    tall = PLANE_ROWS * rows
    dma = pltpu.SemaphoreType.DMA

    def spread(values):
        return values[:, None, None]

    normed = pl.pallas_call(
        exchange_kernel,
        out_shape=jax.ShapeDtypeStruct((channels, rows, cols), jnp.bfloat16),
        in_specs=[pl.BlockSpec(memory_space=pl.ANY), vmem(), vmem()],
        out_specs=vmem(),
        scratch_shapes=[
            pltpu.VMEM((channels, rows, cols), jnp.bfloat16),
            dma(()),
            dma(()),
            dma(()),
        ],
        compiler_params=pltpu.CompilerParams(
            collective_id=0, has_side_effects=True, vmem_limit_bytes=VMEM_LIMIT
        ),
        name="exchange",
    )(pair, spread(norm_gain), spread(norm_bias))
    left_edges, right_edges = project_edges(normed, pair_mask, w_edges)
    product_normed = pl.pallas_call(
        functools.partial(triangle_kernel, depth),
        out_shape=jax.ShapeDtypeStruct((hidden, rows, cols), jnp.bfloat16),
        in_specs=[vmem()] * 4,
        out_specs=vmem(),
        scratch_shapes=[
            pltpu.VMEM((mine, tall, width), jnp.bfloat16),
            pltpu.VMEM((mine, depth * tall, width), jnp.bfloat16),
            pltpu.VMEM((2, mine, tall, cols), jnp.bfloat16),
            pltpu.VMEM((hidden, rows, cols), jnp.bfloat16),
            dma((3,)),
            dma((plane, CHUNKS)),
            dma((plane, CHUNKS)),
            dma((plane,)),
            dma((plane,)),
            dma((depth - 1, CHUNKS)),
            dma((depth - 1, CHUNKS)),
            dma((depth - 1, CHUNKS)),
            dma((depth - 1, CHUNKS)),
            dma((plane, CHUNKS)),
            dma((plane, CHUNKS)),
        ],
        compiler_params=pltpu.CompilerParams(
            collective_id=1, has_side_effects=True, vmem_limit_bytes=VMEM_LIMIT
        ),
        name="triangle",
    )(left_edges, right_edges, spread(out_gain), spread(out_bias))
    return finish(normed, product_normed, w_gate, w_out)


def solution(mesh):
    sizes = dict(mesh.shape)
    depth = sizes["res"] // PLANE_ROWS
    body = wide_body
    if sizes["chan"] == 2 and sizes["res"] % PLANE_ROWS == 0 and depth in (2, 4):
        body = functools.partial(plane_body, depth)
    return jax.shard_map(
        body,
        mesh=mesh,
        in_specs=(
            P(("groups", "chan"), "res", None),
            P(("groups", "res"), "chan"),
            P(),
            P(),
            P(),
            P(),
            P(),
            P(),
            P(),
        ),
        out_specs=P("groups", "res", "chan"),
        check_vma=False,
    )
```

```python
import functools

import jax
import jax.numpy as jnp
from jax import lax
from jax.experimental import pallas as pl
from jax.experimental.pallas import tpu as pltpu
from jax.sharding import PartitionSpec as P

epsilon = 1e-05
MESH = pl.DeviceIdType.MESH
PLANE_ROWS = 4
CHUNKS = 4
UNROLL = 2
VMEM_LIMIT = 48 * 1024 * 1024


def layer_norm(values, scale_gain, shift_bias):
    average = jnp.mean(values, axis=0, keepdims=True)
    centered = values - average
    variance = jnp.mean(centered * centered, axis=0, keepdims=True)
    return (
        centered * lax.rsqrt(variance + epsilon) * scale_gain[:, None, None]
        + shift_bias[:, None, None]
    )


def project_edges(normed, mask_block, w_edges):
    hidden = w_edges.shape[1] // 4
    maskf = mask_block.astype(jnp.float32)[None]

    def edge_half(offset):
        gate_part = jnp.einsum(
            "cij,ch->hij",
            normed,
            w_edges[:, offset : offset + hidden],
            preferred_element_type=jnp.float32,
        )
        value_part = jnp.einsum(
            "cij,ch->hij",
            normed,
            w_edges[:, offset + hidden : offset + 2 * hidden],
            preferred_element_type=jnp.float32,
        )
        return (jax.nn.sigmoid(gate_part) * value_part * maskf).astype(jnp.bfloat16)

    return (edge_half(0), edge_half(2 * hidden))


def finish(normed, product_normed, w_gate, w_out):
    gate_values = jax.nn.sigmoid(
        jnp.einsum("cij,cd->dij", normed, w_gate, preferred_element_type=jnp.float32)
    )
    mixed_out = jnp.einsum("hij,hd->dij", product_normed, w_out, preferred_element_type=jnp.float32)
    return (gate_values * mixed_out).astype(jnp.bfloat16)


def wide_body(pair, pair_mask, norm_gain, norm_bias, w_edges, w_gate, out_gain, out_bias, w_out):
    quarter = pair_mask.shape[1]
    whole_rows, mask_rows = (
        lax.all_gather(pair, "chan", axis=0, tiled=True),
        lax.all_gather(pair_mask, "chan", axis=1, tiled=True),
    )
    normed_rows = layer_norm(whole_rows.astype(jnp.float32), norm_gain, norm_bias).astype(
        jnp.bfloat16
    )
    left_edges, right_edges = project_edges(normed_rows, mask_rows, w_edges)
    left_edges, right_edges = (
        lax.all_to_all(left_edges, "res", split_axis=0, concat_axis=1, tiled=True),
        lax.all_to_all(right_edges, "res", split_axis=0, concat_axis=1, tiled=True),
    )
    right_slice = lax.dynamic_slice_in_dim(
        right_edges, lax.axis_index("chan") * quarter, quarter, 1
    )
    product = jnp.einsum(
        "cik,cjk->cij", left_edges, right_slice, preferred_element_type=jnp.float32
    )
    normed = lax.dynamic_slice_in_dim(normed_rows, lax.axis_index("chan") * quarter, quarter, 2)
    returned = lax.all_to_all(
        product.astype(jnp.bfloat16), "res", split_axis=1, concat_axis=0, tiled=True
    )
    product_normed = layer_norm(returned.astype(jnp.float32), out_gain, out_bias).astype(
        jnp.bfloat16
    )
    return finish(normed, product_normed, w_gate, w_out)


def centre(source):
    values = source.astype(jnp.float32)
    average = jnp.mean(values, axis=0, keepdims=True)
    centered = values - average
    variance = jnp.mean(centered * centered, axis=0, keepdims=True)
    return centered * lax.rsqrt(variance + epsilon)


def triangle_kernel(
    depth,
    pair_ref,
    mask_ref,
    columns_ref,
    edges_ref,
    gate_ref,
    last_ref,
    out_ref,
    whole,
    mask,
    columns,
    edges,
    gate_weight,
    last_weight,
    edges_t,
    gate_t,
    last_t,
    wide,
    scaled,
    staged,
    normed,
    gates,
    left_ref,
    right_ref,
    lefts,
    rights,
    products,
    returned,
    local_sem,
    load_sem,
    pair_send,
    pair_recv,
    right_send,
    right_recv,
    left_send,
    left_recv,
    up_send,
    up_recv,
    down_send,
    down_recv,
    back_send,
    back_recv,
):
    groups, res, x = lax.axis_index("groups"), lax.axis_index("res"), lax.axis_index("chan")
    z, r = res // PLANE_ROWS, res % PLANE_ROWS
    plane = 2 * PLANE_ROWS
    p = r * 2 + x
    rows, cols = left_ref.shape[1], left_ref.shape[2]
    half = pair_ref.shape[0]
    channels, hidden = normed.shape[1], left_ref.shape[0]
    mine = left_ref.shape[0] // plane
    step = mine // CHUNKS
    tall = PLANE_ROWS * rows

    loads = [
        pltpu.make_async_copy(source, target, load_sem.at[index])
        for index, (source, target) in enumerate(
            (
                (columns_ref, columns),
                (edges_ref, edges),
                (gate_ref, gate_weight),
                (last_ref, last_weight),
                (mask_ref, mask),
            )
        )
    ]
    place = whole.at[pl.ds(x * half, half)]
    own_pair = pltpu.make_async_copy(
        pair_ref.at[:, :, pl.ds(pl.multiple_of(x * cols, cols), cols)], place, local_sem.at[3]
    )
    own_pair.start()
    for load in loads:
        load.start()

    def device(q):
        return (groups, z * PLANE_ROWS + q // 2, q % 2)

    def peer(offset):
        return (p + offset) % plane

    barrier = pltpu.get_barrier_semaphore()

    def greet(offset, carry):
        pl.semaphore_signal(barrier, inc=1, device_id=device(peer(offset)), device_id_type=MESH)
        return carry

    lax.fori_loop(1, plane, greet, 0)

    @pl.when(z < depth - 1)
    def _():
        pl.semaphore_signal(
            barrier, inc=1, device_id=(groups, res + PLANE_ROWS, x), device_id_type=MESH
        )

    @pl.when(z > 0)
    def _():
        pl.semaphore_signal(
            barrier, inc=1, device_id=(groups, res - PLANE_ROWS, x), device_id_type=MESH
        )

    beside = jnp.where(z < depth - 1, 1, 0) + jnp.where(z > 0, 1, 0)
    pl.semaphore_wait(barrier, plane - 1 + beside)

    other = 1 - x
    swap = pltpu.make_async_remote_copy(
        src_ref=pair_ref.at[:, :, pl.ds(pl.multiple_of(other * cols, cols), cols)],
        dst_ref=place,
        send_sem=pair_send,
        recv_sem=pair_recv,
        device_id=(groups, res, other),
        device_id_type=MESH,
    )
    swap.start()
    for load in loads:
        load.wait()
    for index in range(4):
        wide[index] = jnp.broadcast_to(columns[:, index : index + 1], wide.shape[1:])
    edges_t[...] = edges[...].T
    gate_t[...] = gate_weight[...].T
    last_t[...] = last_weight[...].T
    own_pair.wait()
    swap.wait_recv()
    scaled[...] = centre(whole[...]).reshape(scaled.shape)

    def line(i, count):
        return pl.ds(i, count, stride=rows)

    def project(i, offset):
        parts = jnp.dot(
            edges_t[offset : offset + 2 * hidden, :], normed[i], preferred_element_type=jnp.float32
        )
        valid = mask[pl.ds(i, 1), :].astype(jnp.float32)
        staged[line(i, hidden), :] = jax.nn.sigmoid(parts[:hidden]) * parts[hidden:] * valid

    def right_row(i, carry):
        values = scaled[line(i, channels), :] * wide[0] + wide[1]
        normed[i] = values.astype(normed.dtype)
        project(i, 2 * hidden)
        return carry

    def left_row(i, carry):
        project(i, 0)
        return carry

    def gate_row(i, carry):
        gates[i] = jax.nn.sigmoid(
            jnp.dot(gate_t[...], normed[i], preferred_element_type=jnp.float32)
        )
        return carry

    lax.fori_loop(0, rows, right_row, 0, unroll=UNROLL)
    right_ref[...] = staged[...].reshape(right_ref.shape).astype(right_ref.dtype)

    here = pl.ds(pl.multiple_of(z * tall + r * rows, rows), rows)
    here_left = pl.ds(pl.multiple_of(r * rows, rows), rows)
    here_cols = pl.ds(pl.multiple_of(x * cols, cols), cols)

    def right_copy(offset, c):
        q = peer(offset)
        return pltpu.make_async_remote_copy(
            src_ref=right_ref.at[pl.ds(q * mine + c * step, step)],
            dst_ref=rights.at[pl.ds(c * step, step), here, here_cols],
            send_sem=right_send.at[offset, c],
            recv_sem=right_recv.at[offset, c],
            device_id=device(q),
            device_id_type=MESH,
        )

    def left_copy(offset):
        q = peer(offset)
        return pltpu.make_async_remote_copy(
            src_ref=left_ref.at[pl.ds(q * mine, mine)],
            dst_ref=lefts.at[:, here_left, here_cols],
            send_sem=left_send.at[offset],
            recv_sem=left_recv.at[offset],
            device_id=device(q),
            device_id_type=MESH,
        )

    own_right = pltpu.make_async_copy(
        right_ref.at[pl.ds(p * mine, mine)], rights.at[:, here, here_cols], local_sem.at[0]
    )
    own_left = pltpu.make_async_copy(
        left_ref.at[pl.ds(p * mine, mine)], lefts.at[:, here_left, here_cols], local_sem.at[1]
    )
    own_right.start()

    def over_peers(act):
        def one(offset, carry):
            act(offset)
            return carry

        lax.fori_loop(1, plane, one, 0)

    for c in range(CHUNKS):
        over_peers(lambda offset: right_copy(offset, c).start())
    lax.fori_loop(0, rows, left_row, 0, unroll=UNROLL)
    left_ref[...] = staged[...].reshape(left_ref.shape).astype(left_ref.dtype)
    own_left.start()
    over_peers(lambda offset: left_copy(offset).start())

    def hop(owner, c, upward, distance):
        block = rights.at[
            pl.ds(c * step, step), pl.ds(pl.multiple_of(owner * tall, tall), tall), :
        ]
        send, recv = (up_send, up_recv) if upward else (down_send, down_recv)
        return pltpu.make_async_remote_copy(
            src_ref=block,
            dst_ref=block,
            send_sem=send.at[distance, c],
            recv_sem=recv.at[distance, c],
            device_id=(groups, res + PLANE_ROWS if upward else res - PLANE_ROWS, x),
            device_id_type=MESH,
        )

    own_right.wait()
    for c in range(CHUNKS):
        over_peers(lambda offset: right_copy(offset, c).wait_recv())

        @pl.when(z < depth - 1)
        def _():
            hop(z, c, True, 0).start()

        @pl.when(z > 0)
        def _():
            hop(z, c, False, 0).start()

    lax.fori_loop(0, rows, gate_row, 0, unroll=UNROLL)

    def pass_on(distance, c):
        @pl.when(z >= distance)
        def _():
            hop(z - distance, c, True, distance - 1).wait_recv()

        @pl.when((z >= distance) & (z < depth - 1))
        def _():
            hop(z - distance, c, True, distance).start()

        @pl.when(z + distance < depth)
        def _():
            hop(z + distance, c, False, distance - 1).wait_recv()

        @pl.when((z + distance < depth) & (z > 0))
        def _():
            hop(z + distance, c, False, distance).start()

    near = z // (depth // 2)

    def back_copy(r_to, side, c):
        q = r_to * 2 + side
        offset = (q - p + plane) % plane
        return pltpu.make_async_remote_copy(
            src_ref=products.at[
                side, pl.ds(c * step, step), pl.ds(pl.multiple_of(r_to * rows, rows), rows), :
            ],
            dst_ref=returned.at[pl.ds(p * mine + c * step, step)],
            send_sem=back_send.at[offset, c],
            recv_sem=back_recv.at[offset, c],
            device_id=device(q),
            device_id_type=MESH,
        )

    def multiply(side, c):
        part = pl.ds(c * step, step)
        result = lax.dot_general(
            lefts[part],
            rights[part, pl.ds(pl.multiple_of(side * cols, cols), cols), :],
            (((2,), (2,)), ((0,), (0,))),
            preferred_element_type=jnp.float32,
        )
        products[side, part] = result.astype(products.dtype)

        def give(r_to, carry):
            @pl.when(r_to * 2 + side != p)
            def _():
                back_copy(r_to, side, c).start()

            return carry

        lax.fori_loop(0, PLANE_ROWS, give, 0)

    for c in range(CHUNKS):
        pass_on(1, c)
    own_left.wait()
    over_peers(lambda offset: left_copy(offset).wait_recv())
    for c in range(CHUNKS):
        multiply(near, c)
    for c in range(CHUNKS):
        for distance in range(2, depth):
            pass_on(distance, c)
        multiply(1 - near, c)

    own_back = pltpu.make_async_copy(
        products.at[x, :, here_left, :], returned.at[pl.ds(p * mine, mine)], local_sem.at[2]
    )
    own_back.start()
    own_back.wait()

    def back_wait(offset, c, receive):
        q = peer(offset)
        copy = back_copy(q // 2, q % 2, c)
        if receive:
            copy.wait_recv()
        else:
            copy.wait_send()

    for c in range(CHUNKS):
        over_peers(lambda offset: back_wait(offset, c, True))
    scaled[...] = centre(returned[...]).reshape(scaled.shape)

    def last_row(i, carry):
        values = scaled[line(i, hidden), :] * wide[2] + wide[3]
        mixed = jnp.dot(
            last_t[...], values.astype(jnp.bfloat16), preferred_element_type=jnp.float32
        )
        staged[line(i, channels), :] = gates[i] * mixed
        return carry

    lax.fori_loop(0, rows, last_row, 0, unroll=UNROLL)
    out_ref[...] = staged[...].reshape(out_ref.shape).astype(out_ref.dtype)

    for c in range(CHUNKS):
        over_peers(lambda offset: back_wait(offset, c, False))
        over_peers(lambda offset: right_copy(offset, c).wait_send())
        for distance in range(depth - 1):

            @pl.when((z >= distance) & (z < depth - 1))
            def _():
                hop(z - distance, c, True, distance).wait_send()

            @pl.when((z + distance < depth) & (z > 0))
            def _():
                hop(z + distance, c, False, distance).wait_send()

    over_peers(lambda offset: left_copy(offset).wait_send())
    swap.wait_send()


def plane_body(
    depth, pair, pair_mask, norm_gain, norm_bias, w_edges, w_gate, out_gain, out_bias, w_out
):
    rows, cols = pair_mask.shape
    channels, hidden = w_gate.shape[0], w_out.shape[0]
    width = 2 * cols
    plane = 2 * PLANE_ROWS
    mine = hidden // plane
    tall = PLANE_ROWS * rows
    dma = pltpu.SemaphoreType.DMA

    columns = jnp.stack([norm_gain, norm_bias, out_gain, out_bias], axis=1)
    bf16, f32 = jnp.bfloat16, jnp.float32
    return pl.pallas_call(
        functools.partial(triangle_kernel, depth),
        out_shape=jax.ShapeDtypeStruct((channels, rows, cols), bf16),
        in_specs=[pl.BlockSpec(memory_space=pltpu.HBM)] * 6,
        out_specs=pl.BlockSpec(memory_space=pltpu.VMEM),
        scratch_shapes=[
            pltpu.VMEM((channels, rows, cols), bf16),
            pltpu.VMEM(pair_mask.shape, pair_mask.dtype),
            pltpu.VMEM(columns.shape, f32),
            pltpu.VMEM(w_edges.shape, bf16),
            pltpu.VMEM(w_gate.shape, bf16),
            pltpu.VMEM(w_out.shape, bf16),
            pltpu.VMEM(w_edges.shape[::-1], bf16),
            pltpu.VMEM(w_gate.shape[::-1], bf16),
            pltpu.VMEM(w_out.shape[::-1], bf16),
            pltpu.VMEM((4, channels, cols), f32),
            pltpu.VMEM((channels * rows, cols), f32),
            pltpu.VMEM((hidden * rows, cols), f32),
            pltpu.VMEM((rows, channels, cols), bf16),
            pltpu.VMEM((rows, channels, cols), f32),
            pltpu.VMEM((hidden, rows, cols), bf16),
            pltpu.VMEM((hidden, rows, cols), bf16),
            pltpu.VMEM((mine, tall, width), bf16),
            pltpu.VMEM((mine, depth * tall, width), bf16),
            pltpu.VMEM((2, mine, tall, cols), bf16),
            pltpu.VMEM((hidden, rows, cols), bf16),
            dma((4,)),
            dma((5,)),
            dma(()),
            dma(()),
            dma((plane, CHUNKS)),
            dma((plane, CHUNKS)),
            dma((plane,)),
            dma((plane,)),
            dma((depth - 1, CHUNKS)),
            dma((depth - 1, CHUNKS)),
            dma((depth - 1, CHUNKS)),
            dma((depth - 1, CHUNKS)),
            dma((plane, CHUNKS)),
            dma((plane, CHUNKS)),
        ],
        compiler_params=pltpu.CompilerParams(
            collective_id=1, has_side_effects=True, vmem_limit_bytes=VMEM_LIMIT
        ),
        name="triangle",
    )(pair, pair_mask, columns, w_edges, w_gate, w_out)


def solution(mesh):
    sizes = dict(mesh.shape)
    depth = sizes["res"] // PLANE_ROWS
    body = wide_body
    if sizes["chan"] == 2 and sizes["res"] % PLANE_ROWS == 0 and depth in (2, 4):
        body = functools.partial(plane_body, depth)
    return jax.shard_map(
        body,
        mesh=mesh,
        in_specs=(
            P(("groups", "chan"), "res", None),
            P(("groups", "res"), "chan"),
            P(),
            P(),
            P(),
            P(),
            P(),
            P(),
            P(),
        ),
        out_specs=P("groups", "res", "chan"),
        check_vma=False,
    )
```

```python
import functools

import jax
import jax.numpy as jnp
from jax import lax
from jax.experimental import pallas as pl
from jax.experimental.pallas import tpu as pltpu
from jax.sharding import PartitionSpec as P

epsilon = 1e-05
MESH = pl.DeviceIdType.MESH
PLANE_ROWS = 4
CHUNKS = 4
UNROLL = 2
VMEM_LIMIT = 60 * 1024 * 1024


def layer_norm(values, scale_gain, shift_bias):
    average = jnp.mean(values, axis=0, keepdims=True)
    centered = values - average
    variance = jnp.mean(centered * centered, axis=0, keepdims=True)
    return (
        centered * lax.rsqrt(variance + epsilon) * scale_gain[:, None, None]
        + shift_bias[:, None, None]
    )


def project_edges(normed, mask_block, w_edges):
    hidden = w_edges.shape[1] // 4
    maskf = mask_block.astype(jnp.float32)[None]

    def edge_half(offset):
        gate_part = jnp.einsum(
            "cij,ch->hij",
            normed,
            w_edges[:, offset : offset + hidden],
            preferred_element_type=jnp.float32,
        )
        value_part = jnp.einsum(
            "cij,ch->hij",
            normed,
            w_edges[:, offset + hidden : offset + 2 * hidden],
            preferred_element_type=jnp.float32,
        )
        return (jax.nn.sigmoid(gate_part) * value_part * maskf).astype(jnp.bfloat16)

    return (edge_half(0), edge_half(2 * hidden))


def finish(normed, product_normed, w_gate, w_out):
    gate_values = jax.nn.sigmoid(
        jnp.einsum("cij,cd->dij", normed, w_gate, preferred_element_type=jnp.float32)
    )
    mixed_out = jnp.einsum("hij,hd->dij", product_normed, w_out, preferred_element_type=jnp.float32)
    return (gate_values * mixed_out).astype(jnp.bfloat16)


def wide_body(pair, pair_mask, norm_gain, norm_bias, w_edges, w_gate, out_gain, out_bias, w_out):
    quarter = pair_mask.shape[1]
    whole_rows, mask_rows = (
        lax.all_gather(pair, "chan", axis=0, tiled=True),
        lax.all_gather(pair_mask, "chan", axis=1, tiled=True),
    )
    normed_rows = layer_norm(whole_rows.astype(jnp.float32), norm_gain, norm_bias).astype(
        jnp.bfloat16
    )
    left_edges, right_edges = project_edges(normed_rows, mask_rows, w_edges)
    left_edges, right_edges = (
        lax.all_to_all(left_edges, "res", split_axis=0, concat_axis=1, tiled=True),
        lax.all_to_all(right_edges, "res", split_axis=0, concat_axis=1, tiled=True),
    )
    right_slice = lax.dynamic_slice_in_dim(
        right_edges, lax.axis_index("chan") * quarter, quarter, 1
    )
    product = jnp.einsum(
        "cik,cjk->cij", left_edges, right_slice, preferred_element_type=jnp.float32
    )
    normed = lax.dynamic_slice_in_dim(normed_rows, lax.axis_index("chan") * quarter, quarter, 2)
    returned = lax.all_to_all(
        product.astype(jnp.bfloat16), "res", split_axis=1, concat_axis=0, tiled=True
    )
    product_normed = layer_norm(returned.astype(jnp.float32), out_gain, out_bias).astype(
        jnp.bfloat16
    )
    return finish(normed, product_normed, w_gate, w_out)


def centre(source):
    values = source.astype(jnp.float32)
    average = jnp.mean(values, axis=0, keepdims=True)
    centered = values - average
    variance = jnp.mean(centered * centered, axis=0, keepdims=True)
    return centered * lax.rsqrt(variance + epsilon)


def triangle_kernel(
    pair_ref,
    mask_ref,
    columns_ref,
    edges_ref,
    gate_ref,
    last_ref,
    out_ref,
    whole,
    mask,
    columns,
    edges,
    gate_weight,
    last_weight,
    edges_t,
    gate_t,
    last_t,
    wide,
    scaled,
    staged,
    normed,
    gates,
    left_ref,
    right_ref,
    lefts,
    rights,
    products,
    returned,
    local_sem,
    load_sem,
    pair_send,
    pair_recv,
    right_send,
    right_recv,
    left_send,
    left_recv,
    hop_send,
    hop_recv,
    back_send,
    back_recv,
):
    groups, res, x = lax.axis_index("groups"), lax.axis_index("res"), lax.axis_index("chan")
    z, r = res // PLANE_ROWS, res % PLANE_ROWS
    plane = 2 * PLANE_ROWS
    p = r * 2 + x
    rows, cols = left_ref.shape[1], left_ref.shape[2]
    half = pair_ref.shape[0]
    channels, hidden = normed.shape[1], left_ref.shape[0]
    mine = left_ref.shape[0] // plane
    step = mine // CHUNKS
    tall = PLANE_ROWS * rows

    loads = [
        pltpu.make_async_copy(source, target, load_sem.at[index])
        for index, (source, target) in enumerate(
            (
                (columns_ref, columns),
                (edges_ref, edges),
                (gate_ref, gate_weight),
                (last_ref, last_weight),
                (mask_ref, mask),
            )
        )
    ]
    place = whole.at[pl.ds(x * half, half)]
    own_pair = pltpu.make_async_copy(
        pair_ref.at[:, :, pl.ds(pl.multiple_of(x * cols, cols), cols)], place, local_sem.at[3]
    )
    own_pair.start()
    for load in loads:
        load.start()

    pod = z // 2
    hub_z, end_z = 1 + pod, 3 * pod
    is_hub = z == hub_z
    kind = jnp.where(is_hub, 0, 1)
    first = jnp.where(is_hub, 1, 0)

    def device(q, plane_z):
        return (groups, plane_z * PLANE_ROWS + q // 2, q % 2)

    def peer(offset):
        return (p + offset) % plane

    barrier = pltpu.get_barrier_semaphore()

    def signal(target):
        pl.semaphore_signal(barrier, inc=1, device_id=target, device_id_type=MESH)

    def greet(offset, carry):
        signal(device(peer(offset), hub_z))
        return carry

    def greet_end(offset, carry):
        signal(device(peer(offset), end_z))
        return carry

    lax.fori_loop(first, plane, greet, 0)

    @pl.when(is_hub)
    def _():
        lax.fori_loop(0, plane, greet_end, 0)
        signal(device(p, 3 - hub_z))

    @pl.when(z == end_z)
    def _():
        signal((groups, res, 1 - x))

    pl.semaphore_wait(barrier, jnp.where(is_hub, 2 * plane, plane + 1))

    other = 1 - x
    swap = pltpu.make_async_remote_copy(
        src_ref=pair_ref.at[:, :, pl.ds(pl.multiple_of(other * cols, cols), cols)],
        dst_ref=place,
        send_sem=pair_send,
        recv_sem=pair_recv,
        device_id=(groups, res, other),
        device_id_type=MESH,
    )
    swap.start()
    for load in loads:
        load.wait()
    for index in range(4):
        wide[index] = jnp.broadcast_to(columns[:, index : index + 1], wide.shape[1:])
    edges_t[...] = edges[...].T
    gate_t[...] = gate_weight[...].T
    last_t[...] = last_weight[...].T
    own_pair.wait()
    swap.wait_recv()
    scaled[...] = centre(whole[...]).reshape(scaled.shape)

    def line(i, count):
        return pl.ds(i, count, stride=rows)

    def project(i, offset):
        parts = jnp.dot(
            edges_t[offset : offset + 2 * hidden, :], normed[i], preferred_element_type=jnp.float32
        )
        valid = mask[pl.ds(i, 1), :].astype(jnp.float32)
        staged[line(i, hidden), :] = jax.nn.sigmoid(parts[:hidden]) * parts[hidden:] * valid

    def right_row(i, carry):
        values = scaled[line(i, channels), :] * wide[0] + wide[1]
        normed[i] = values.astype(normed.dtype)
        project(i, 2 * hidden)
        return carry

    def left_row(i, carry):
        project(i, 0)
        return carry

    def gate_row(i, carry):
        gates[i] = jax.nn.sigmoid(
            jnp.dot(gate_t[...], normed[i], preferred_element_type=jnp.float32)
        )
        return carry

    lax.fori_loop(0, rows, right_row, 0, unroll=UNROLL)
    right_ref[...] = staged[...].reshape(right_ref.shape).astype(right_ref.dtype)

    here = pl.ds(pl.multiple_of(z * tall + r * rows, rows), rows)
    here_left = pl.ds(pl.multiple_of(r * rows, rows), rows)
    here_cols = pl.ds(pl.multiple_of(x * cols, cols), cols)

    def right_copy(offset, c, sender):
        q = peer(offset)
        return pltpu.make_async_remote_copy(
            src_ref=right_ref.at[pl.ds(q * mine + c * step, step)],
            dst_ref=rights.at[pl.ds(c * step, step), here, here_cols],
            send_sem=right_send.at[offset, c],
            recv_sem=right_recv.at[sender, offset, c],
            device_id=device(q, hub_z),
            device_id_type=MESH,
        )

    def left_copy(offset, sender):
        q = peer(offset)
        return pltpu.make_async_remote_copy(
            src_ref=left_ref.at[pl.ds(q * mine, mine)],
            dst_ref=lefts.at[kind, :, here_left, here_cols],
            send_sem=left_send.at[offset],
            recv_sem=left_recv.at[sender, offset],
            device_id=device(q, hub_z),
            device_id_type=MESH,
        )

    own_right = pltpu.make_async_copy(
        right_ref.at[pl.ds(p * mine, mine)], rights.at[:, here, here_cols], local_sem.at[0]
    )
    own_left = pltpu.make_async_copy(
        left_ref.at[pl.ds(p * mine, mine)], lefts.at[0, :, here_left, here_cols], local_sem.at[1]
    )

    def over_peers(start, act):
        def one(offset, carry):
            act(offset)
            return carry

        lax.fori_loop(start, plane, one, 0)

    for c in range(CHUNKS):
        over_peers(first, lambda offset: right_copy(offset, c, kind).start())

    @pl.when(is_hub)
    def _():
        own_right.start()

    lax.fori_loop(0, rows, left_row, 0, unroll=UNROLL)
    left_ref[...] = staged[...].reshape(left_ref.shape).astype(left_ref.dtype)
    over_peers(first, lambda offset: left_copy(offset, kind).start())

    def hop(owner, c, sender):
        block = rights.at[
            pl.ds(c * step, step), pl.ds(pl.multiple_of(owner * tall, tall), tall), :
        ]
        return pltpu.make_async_remote_copy(
            src_ref=block,
            dst_ref=block,
            send_sem=hop_send.at[sender, c],
            recv_sem=hop_recv.at[sender, c],
            device_id=device(p, 3 - hub_z),
            device_id_type=MESH,
        )

    @pl.when(is_hub)
    def _():
        own_left.start()
        own_right.wait()
        for c in range(CHUNKS):
            over_peers(1, lambda offset: right_copy(offset, c, 0).wait_recv())
            hop(hub_z, c, 0).start()

    lax.fori_loop(0, rows, gate_row, 0, unroll=UNROLL)

    def back_copy(member, r_to, side, c):
        q = r_to * 2 + side
        offset = (q - p + plane) % plane
        return pltpu.make_async_remote_copy(
            src_ref=products.at[
                member,
                side,
                pl.ds(c * step, step),
                pl.ds(pl.multiple_of(r_to * rows, rows), rows),
                :,
            ],
            dst_ref=returned.at[pl.ds(p * mine + c * step, step)],
            send_sem=back_send.at[member, offset, c],
            recv_sem=back_recv.at[offset, c],
            device_id=device(q, end_z if member else hub_z),
            device_id_type=MESH,
        )

    def multiply(member, side, c):
        part = pl.ds(c * step, step)
        result = lax.dot_general(
            lefts[member, part],
            rights[part, pl.ds(pl.multiple_of(side * cols, cols), cols), :],
            (((2,), (2,)), ((0,), (0,))),
            preferred_element_type=jnp.float32,
        )
        products[member, side, part] = result.astype(products.dtype)

        def give(r_to, carry):
            if member:
                back_copy(member, r_to, side, c).start()
            else:

                @pl.when(r_to * 2 + side != p)
                def _():
                    back_copy(member, r_to, side, c).start()

            return carry

        lax.fori_loop(0, PLANE_ROWS, give, 0)

    own_back = pltpu.make_async_copy(
        products.at[0, x, :, here_left, :], returned.at[pl.ds(p * mine, mine)], local_sem.at[2]
    )

    @pl.when(is_hub)
    def _():
        for c in range(CHUNKS):
            over_peers(0, lambda offset: right_copy(offset, c, 1).wait_recv())
            hop(end_z, c, 1).start()
        own_left.wait()
        over_peers(1, lambda offset: left_copy(offset, 0).wait_recv())
        for c in range(CHUNKS):
            multiply(0, pod, c)
        over_peers(0, lambda offset: left_copy(offset, 1).wait_recv())
        for c in range(CHUNKS):
            multiply(1, pod, c)
        for c in range(CHUNKS):
            hop(3 - hub_z, c, 0).wait_recv()
            hop(3 - end_z, c, 1).wait_recv()
            multiply(1, 1 - pod, c)
            multiply(0, 1 - pod, c)
        own_back.start()
        own_back.wait()

    def back_of(member, offset, c):
        q = peer(offset)
        return back_copy(member, q // 2, q % 2, c)

    for c in range(CHUNKS):
        over_peers(first, lambda offset: back_of(0, offset, c).wait_recv())
    scaled[...] = centre(returned[...]).reshape(scaled.shape)

    def last_row(i, carry):
        values = scaled[line(i, hidden), :] * wide[2] + wide[3]
        mixed = jnp.dot(
            last_t[...], values.astype(jnp.bfloat16), preferred_element_type=jnp.float32
        )
        staged[line(i, channels), :] = gates[i] * mixed
        return carry

    lax.fori_loop(0, rows, last_row, 0, unroll=UNROLL)
    out_ref[...] = staged[...].reshape(out_ref.shape).astype(out_ref.dtype)

    for c in range(CHUNKS):
        over_peers(first, lambda offset: right_copy(offset, c, kind).wait_send())

        @pl.when(is_hub)
        def _():
            over_peers(1, lambda offset: back_of(0, offset, c).wait_send())
            over_peers(0, lambda offset: back_of(1, offset, c).wait_send())
            hop(hub_z, c, 0).wait_send()
            hop(end_z, c, 1).wait_send()

    over_peers(first, lambda offset: left_copy(offset, kind).wait_send())
    swap.wait_send()


def plane_body(
    depth, pair, pair_mask, norm_gain, norm_bias, w_edges, w_gate, out_gain, out_bias, w_out
):
    rows, cols = pair_mask.shape
    channels, hidden = w_gate.shape[0], w_out.shape[0]
    width = 2 * cols
    plane = 2 * PLANE_ROWS
    mine = hidden // plane
    tall = PLANE_ROWS * rows
    dma = pltpu.SemaphoreType.DMA

    columns = jnp.stack([norm_gain, norm_bias, out_gain, out_bias], axis=1)
    bf16, f32 = jnp.bfloat16, jnp.float32
    return pl.pallas_call(
        triangle_kernel,
        out_shape=jax.ShapeDtypeStruct((channels, rows, cols), bf16),
        in_specs=[pl.BlockSpec(memory_space=pltpu.HBM)] * 6,
        out_specs=pl.BlockSpec(memory_space=pltpu.VMEM),
        scratch_shapes=[
            pltpu.VMEM((channels, rows, cols), bf16),
            pltpu.VMEM(pair_mask.shape, pair_mask.dtype),
            pltpu.VMEM(columns.shape, f32),
            pltpu.VMEM(w_edges.shape, bf16),
            pltpu.VMEM(w_gate.shape, bf16),
            pltpu.VMEM(w_out.shape, bf16),
            pltpu.VMEM(w_edges.shape[::-1], bf16),
            pltpu.VMEM(w_gate.shape[::-1], bf16),
            pltpu.VMEM(w_out.shape[::-1], bf16),
            pltpu.VMEM((4, channels, cols), f32),
            pltpu.VMEM((channels * rows, cols), f32),
            pltpu.VMEM((hidden * rows, cols), f32),
            pltpu.VMEM((rows, channels, cols), bf16),
            pltpu.VMEM((rows, channels, cols), f32),
            pltpu.VMEM((hidden, rows, cols), bf16),
            pltpu.VMEM((hidden, rows, cols), bf16),
            pltpu.VMEM((2, mine, tall, width), bf16),
            pltpu.VMEM((mine, depth * tall, width), bf16),
            pltpu.VMEM((2, 2, mine, tall, cols), bf16),
            pltpu.VMEM((hidden, rows, cols), bf16),
            dma((4,)),
            dma((5,)),
            dma(()),
            dma(()),
            dma((plane, CHUNKS)),
            dma((2, plane, CHUNKS)),
            dma((plane,)),
            dma((2, plane)),
            dma((2, CHUNKS)),
            dma((2, CHUNKS)),
            dma((2, plane, CHUNKS)),
            dma((plane, CHUNKS)),
        ],
        compiler_params=pltpu.CompilerParams(
            collective_id=1, has_side_effects=True, vmem_limit_bytes=VMEM_LIMIT
        ),
        name="triangle",
    )(pair, pair_mask, columns, w_edges, w_gate, w_out)


def solution(mesh):
    sizes = dict(mesh.shape)
    depth = sizes["res"] // PLANE_ROWS
    body = wide_body
    if sizes["chan"] == 2 and sizes["res"] % PLANE_ROWS == 0 and depth == 4:
        body = functools.partial(plane_body, depth)
    return jax.shard_map(
        body,
        mesh=mesh,
        in_specs=(
            P(("groups", "chan"), "res", None),
            P(("groups", "res"), "chan"),
            P(),
            P(),
            P(),
            P(),
            P(),
            P(),
            P(),
        ),
        out_specs=P("groups", "res", "chan"),
        check_vma=False,
    )
```

```python
import functools

import jax
import jax.numpy as jnp
from jax import lax
from jax.experimental import pallas as pl
from jax.experimental.pallas import tpu as pltpu
from jax.sharding import PartitionSpec as P

epsilon = 1e-05
MESH = pl.DeviceIdType.MESH
PLANE_ROWS = 4
CHUNKS = 4
UNROLL = 16
VMEM_LIMIT = 60 * 1024 * 1024


def layer_norm(values, scale_gain, shift_bias):
    average = jnp.mean(values, axis=0, keepdims=True)
    centered = values - average
    variance = jnp.mean(centered * centered, axis=0, keepdims=True)
    return (
        centered * lax.rsqrt(variance + epsilon) * scale_gain[:, None, None]
        + shift_bias[:, None, None]
    )


def project_edges(normed, mask_block, w_edges):
    hidden = w_edges.shape[1] // 4
    maskf = mask_block.astype(jnp.float32)[None]

    def edge_half(offset):
        gate_part = jnp.einsum(
            "cij,ch->hij",
            normed,
            w_edges[:, offset : offset + hidden],
            preferred_element_type=jnp.float32,
        )
        value_part = jnp.einsum(
            "cij,ch->hij",
            normed,
            w_edges[:, offset + hidden : offset + 2 * hidden],
            preferred_element_type=jnp.float32,
        )
        return (jax.nn.sigmoid(gate_part) * value_part * maskf).astype(jnp.bfloat16)

    return (edge_half(0), edge_half(2 * hidden))


def finish(normed, product_normed, w_gate, w_out):
    gate_values = jax.nn.sigmoid(
        jnp.einsum("cij,cd->dij", normed, w_gate, preferred_element_type=jnp.float32)
    )
    mixed_out = jnp.einsum("hij,hd->dij", product_normed, w_out, preferred_element_type=jnp.float32)
    return (gate_values * mixed_out).astype(jnp.bfloat16)


def wide_body(pair, pair_mask, norm_gain, norm_bias, w_edges, w_gate, out_gain, out_bias, w_out):
    quarter = pair_mask.shape[1]
    whole_rows, mask_rows = (
        lax.all_gather(pair, "chan", axis=0, tiled=True),
        lax.all_gather(pair_mask, "chan", axis=1, tiled=True),
    )
    normed_rows = layer_norm(whole_rows.astype(jnp.float32), norm_gain, norm_bias).astype(
        jnp.bfloat16
    )
    left_edges, right_edges = project_edges(normed_rows, mask_rows, w_edges)
    left_edges, right_edges = (
        lax.all_to_all(left_edges, "res", split_axis=0, concat_axis=1, tiled=True),
        lax.all_to_all(right_edges, "res", split_axis=0, concat_axis=1, tiled=True),
    )
    right_slice = lax.dynamic_slice_in_dim(
        right_edges, lax.axis_index("chan") * quarter, quarter, 1
    )
    product = jnp.einsum(
        "cik,cjk->cij", left_edges, right_slice, preferred_element_type=jnp.float32
    )
    normed = lax.dynamic_slice_in_dim(normed_rows, lax.axis_index("chan") * quarter, quarter, 2)
    returned = lax.all_to_all(
        product.astype(jnp.bfloat16), "res", split_axis=1, concat_axis=0, tiled=True
    )
    product_normed = layer_norm(returned.astype(jnp.float32), out_gain, out_bias).astype(
        jnp.bfloat16
    )
    return finish(normed, product_normed, w_gate, w_out)


def centre(source):
    values = source.astype(jnp.float32)
    average = jnp.mean(values, axis=0, keepdims=True)
    centered = values - average
    variance = jnp.mean(centered * centered, axis=0, keepdims=True)
    return centered * lax.rsqrt(variance + epsilon)


def triangle_kernel(
    pair_ref,
    mask_ref,
    norm_gain_ref,
    norm_bias_ref,
    out_gain_ref,
    out_bias_ref,
    edges_ref,
    gate_ref,
    last_ref,
    out_ref,
    whole,
    mask,
    columns,
    edges,
    gate_weight,
    last_weight,
    edges_t,
    gate_t,
    last_t,
    wide,
    scaled,
    staged,
    normed,
    gates,
    left_ref,
    right_ref,
    lefts,
    rights,
    products,
    returned,
    local_sem,
    load_sem,
    pair_send,
    pair_recv,
    right_send,
    right_recv,
    left_send,
    left_recv,
    hop_send,
    hop_recv,
    back_send,
    back_recv,
):
    groups, res, x = lax.axis_index("groups"), lax.axis_index("res"), lax.axis_index("chan")
    z, r = res // PLANE_ROWS, res % PLANE_ROWS
    plane = 2 * PLANE_ROWS
    p = r * 2 + x
    rows, cols = left_ref.shape[1], left_ref.shape[2]
    half = pair_ref.shape[0]
    channels, hidden = normed.shape[1], left_ref.shape[0]
    mine = left_ref.shape[0] // plane
    step = mine // CHUNKS
    tall = PLANE_ROWS * rows

    loads = [
        pltpu.make_async_copy(source, target, load_sem.at[index])
        for index, (source, target) in enumerate(
            (
                (norm_gain_ref, columns.at[0]),
                (norm_bias_ref, columns.at[1]),
                (out_gain_ref, columns.at[2]),
                (out_bias_ref, columns.at[3]),
                (edges_ref, edges),
                (gate_ref, gate_weight),
                (last_ref, last_weight),
                (mask_ref, mask),
            )
        )
    ]
    place = whole.at[pl.ds(x * half, half)]
    own_pair = pltpu.make_async_copy(
        pair_ref.at[:, :, pl.ds(pl.multiple_of(x * cols, cols), cols)], place, local_sem.at[3]
    )
    own_pair.start()
    for load in loads:
        load.start()

    pod = z // 2
    hub_z, end_z = 1 + pod, 3 * pod
    is_hub = z == hub_z
    kind = jnp.where(is_hub, 0, 1)
    first = jnp.where(is_hub, 1, 0)

    def device(q, plane_z):
        return (groups, plane_z * PLANE_ROWS + q // 2, q % 2)

    def peer(offset):
        return (p + offset) % plane

    barrier = pltpu.get_barrier_semaphore()

    def signal(target):
        pl.semaphore_signal(barrier, inc=1, device_id=target, device_id_type=MESH)

    def greet(offset, carry):
        signal(device(peer(offset), hub_z))
        return carry

    def greet_end(offset, carry):
        signal(device(peer(offset), end_z))
        return carry

    lax.fori_loop(first, plane, greet, 0)

    @pl.when(is_hub)
    def _():
        lax.fori_loop(0, plane, greet_end, 0)
        signal(device(p, 3 - hub_z))

    @pl.when(z == end_z)
    def _():
        signal((groups, res, 1 - x))

    pl.semaphore_wait(barrier, jnp.where(is_hub, 2 * plane, plane + 1))

    other = 1 - x
    swap = pltpu.make_async_remote_copy(
        src_ref=pair_ref.at[:, :, pl.ds(pl.multiple_of(other * cols, cols), cols)],
        dst_ref=place,
        send_sem=pair_send,
        recv_sem=pair_recv,
        device_id=(groups, res, other),
        device_id_type=MESH,
    )
    swap.start()
    for load in loads:
        load.wait()
    for index in range(4):
        wide[index] = jnp.broadcast_to(columns[index], wide.shape[:0:-1]).T
    edges_t[...] = edges[...].T
    gate_t[...] = gate_weight[...].T
    last_t[...] = last_weight[...].T
    own_pair.wait()
    swap.wait_recv()
    scaled[...] = centre(whole[...]).reshape(scaled.shape)

    def line(i, count):
        return pl.ds(i, count, stride=rows)

    def project(i, offset):
        parts = jnp.dot(
            edges_t[offset : offset + 2 * hidden, :], normed[i], preferred_element_type=jnp.float32
        )
        valid = mask[pl.ds(i, 1), :].astype(jnp.float32)
        staged[line(i, hidden), :] = jax.nn.sigmoid(parts[:hidden]) * parts[hidden:] * valid

    def right_row(i, carry):
        values = scaled[line(i, channels), :] * wide[0] + wide[1]
        normed[i] = values.astype(normed.dtype)
        project(i, 2 * hidden)
        return carry

    def left_row(i, carry):
        project(i, 0)
        return carry

    def gate_row(i, carry):
        gates[i] = jax.nn.sigmoid(
            jnp.dot(gate_t[...], normed[i], preferred_element_type=jnp.float32)
        )
        return carry

    lax.fori_loop(0, rows, right_row, 0, unroll=UNROLL)
    right_ref[...] = staged[...].reshape(right_ref.shape).astype(right_ref.dtype)

    here = pl.ds(pl.multiple_of(z * tall + r * rows, rows), rows)
    here_left = pl.ds(pl.multiple_of(r * rows, rows), rows)
    here_cols = pl.ds(pl.multiple_of(x * cols, cols), cols)

    def right_copy(offset, c, sender):
        q = peer(offset)
        return pltpu.make_async_remote_copy(
            src_ref=right_ref.at[pl.ds(q * mine + c * step, step)],
            dst_ref=rights.at[pl.ds(c * step, step), here, here_cols],
            send_sem=right_send.at[offset, c],
            recv_sem=right_recv.at[sender, offset, c],
            device_id=device(q, hub_z),
            device_id_type=MESH,
        )

    def left_copy(offset, sender):
        q = peer(offset)
        return pltpu.make_async_remote_copy(
            src_ref=left_ref.at[pl.ds(q * mine, mine)],
            dst_ref=lefts.at[kind, :, here_left, here_cols],
            send_sem=left_send.at[offset],
            recv_sem=left_recv.at[sender, offset],
            device_id=device(q, hub_z),
            device_id_type=MESH,
        )

    own_right = pltpu.make_async_copy(
        right_ref.at[pl.ds(p * mine, mine)], rights.at[:, here, here_cols], local_sem.at[0]
    )
    own_left = pltpu.make_async_copy(
        left_ref.at[pl.ds(p * mine, mine)], lefts.at[0, :, here_left, here_cols], local_sem.at[1]
    )

    def over_peers(start, act):
        def one(offset, carry):
            act(offset)
            return carry

        lax.fori_loop(start, plane, one, 0)

    for c in range(CHUNKS):
        over_peers(first, lambda offset: right_copy(offset, c, kind).start())

    @pl.when(is_hub)
    def _():
        own_right.start()

    lax.fori_loop(0, rows, left_row, 0, unroll=UNROLL)
    left_ref[...] = staged[...].reshape(left_ref.shape).astype(left_ref.dtype)
    over_peers(first, lambda offset: left_copy(offset, kind).start())

    def hop(owner, c, sender):
        block = rights.at[
            pl.ds(c * step, step), pl.ds(pl.multiple_of(owner * tall, tall), tall), :
        ]
        return pltpu.make_async_remote_copy(
            src_ref=block,
            dst_ref=block,
            send_sem=hop_send.at[sender, c],
            recv_sem=hop_recv.at[sender, c],
            device_id=device(p, 3 - hub_z),
            device_id_type=MESH,
        )

    @pl.when(is_hub)
    def _():
        own_left.start()
        own_right.wait()
        for c in range(CHUNKS):
            over_peers(1, lambda offset: right_copy(offset, c, 0).wait_recv())
            hop(hub_z, c, 0).start()

    lax.fori_loop(0, rows, gate_row, 0, unroll=UNROLL)

    def back_copy(member, r_to, side, c):
        q = r_to * 2 + side
        offset = (q - p + plane) % plane
        return pltpu.make_async_remote_copy(
            src_ref=products.at[
                member,
                side,
                pl.ds(c * step, step),
                pl.ds(pl.multiple_of(r_to * rows, rows), rows),
                :,
            ],
            dst_ref=returned.at[pl.ds(p * mine + c * step, step)],
            send_sem=back_send.at[member, offset, c],
            recv_sem=back_recv.at[offset, c],
            device_id=device(q, end_z if member else hub_z),
            device_id_type=MESH,
        )

    def multiply(member, side, c):
        part = pl.ds(c * step, step)
        result = lax.dot_general(
            lefts[member, part],
            rights[part, pl.ds(pl.multiple_of(side * cols, cols), cols), :],
            (((2,), (2,)), ((0,), (0,))),
            preferred_element_type=jnp.float32,
        )
        products[member, side, part] = result.astype(products.dtype)

        def give(r_to, carry):
            if member:
                back_copy(member, r_to, side, c).start()
            else:

                @pl.when(r_to * 2 + side != p)
                def _():
                    back_copy(member, r_to, side, c).start()

            return carry

        lax.fori_loop(0, PLANE_ROWS, give, 0)

    own_back = pltpu.make_async_copy(
        products.at[0, x, :, here_left, :], returned.at[pl.ds(p * mine, mine)], local_sem.at[2]
    )

    @pl.when(is_hub)
    def _():
        for c in range(CHUNKS):
            over_peers(0, lambda offset: right_copy(offset, c, 1).wait_recv())
            hop(end_z, c, 1).start()
        own_left.wait()
        over_peers(1, lambda offset: left_copy(offset, 0).wait_recv())
        for c in range(CHUNKS):
            multiply(0, pod, c)
        over_peers(0, lambda offset: left_copy(offset, 1).wait_recv())
        for c in range(CHUNKS):
            multiply(1, pod, c)
        for c in range(CHUNKS):
            hop(3 - hub_z, c, 0).wait_recv()
            hop(3 - end_z, c, 1).wait_recv()
            multiply(1, 1 - pod, c)
            multiply(0, 1 - pod, c)
        own_back.start()
        own_back.wait()

    def back_of(member, offset, c):
        q = peer(offset)
        return back_copy(member, q // 2, q % 2, c)

    for c in range(CHUNKS):
        over_peers(first, lambda offset: back_of(0, offset, c).wait_recv())
    scaled[...] = centre(returned[...]).reshape(scaled.shape)

    def last_row(i, carry):
        values = scaled[line(i, hidden), :] * wide[2] + wide[3]
        mixed = jnp.dot(
            last_t[...], values.astype(jnp.bfloat16), preferred_element_type=jnp.float32
        )
        staged[line(i, channels), :] = gates[i] * mixed
        return carry

    lax.fori_loop(0, rows, last_row, 0, unroll=UNROLL)
    out_ref[...] = staged[...].reshape(out_ref.shape).astype(out_ref.dtype)

    for c in range(CHUNKS):
        over_peers(first, lambda offset: right_copy(offset, c, kind).wait_send())

        @pl.when(is_hub)
        def _():
            over_peers(1, lambda offset: back_of(0, offset, c).wait_send())
            over_peers(0, lambda offset: back_of(1, offset, c).wait_send())
            hop(hub_z, c, 0).wait_send()
            hop(end_z, c, 1).wait_send()

    over_peers(first, lambda offset: left_copy(offset, kind).wait_send())
    swap.wait_send()


def plane_body(
    depth, pair, pair_mask, norm_gain, norm_bias, w_edges, w_gate, out_gain, out_bias, w_out
):
    rows, cols = pair_mask.shape
    channels, hidden = w_gate.shape[0], w_out.shape[0]
    width = 2 * cols
    plane = 2 * PLANE_ROWS
    mine = hidden // plane
    tall = PLANE_ROWS * rows
    dma = pltpu.SemaphoreType.DMA

    columns = [v[None] for v in (norm_gain, norm_bias, out_gain, out_bias)]
    bf16, f32 = jnp.bfloat16, jnp.float32
    return pl.pallas_call(
        triangle_kernel,
        out_shape=jax.ShapeDtypeStruct((channels, rows, cols), bf16),
        in_specs=[pl.BlockSpec(memory_space=pltpu.HBM)] * 9,
        out_specs=pl.BlockSpec(memory_space=pltpu.VMEM),
        scratch_shapes=[
            pltpu.VMEM((channels, rows, cols), bf16),
            pltpu.VMEM(pair_mask.shape, pair_mask.dtype),
            pltpu.VMEM((4, 1, channels), f32),
            pltpu.VMEM(w_edges.shape, bf16),
            pltpu.VMEM(w_gate.shape, bf16),
            pltpu.VMEM(w_out.shape, bf16),
            pltpu.VMEM(w_edges.shape[::-1], bf16),
            pltpu.VMEM(w_gate.shape[::-1], bf16),
            pltpu.VMEM(w_out.shape[::-1], bf16),
            pltpu.VMEM((4, channels, cols), f32),
            pltpu.VMEM((channels * rows, cols), f32),
            pltpu.VMEM((hidden * rows, cols), f32),
            pltpu.VMEM((rows, channels, cols), bf16),
            pltpu.VMEM((rows, channels, cols), f32),
            pltpu.VMEM((hidden, rows, cols), bf16),
            pltpu.VMEM((hidden, rows, cols), bf16),
            pltpu.VMEM((2, mine, tall, width), bf16),
            pltpu.VMEM((mine, depth * tall, width), bf16),
            pltpu.VMEM((2, 2, mine, tall, cols), bf16),
            pltpu.VMEM((hidden, rows, cols), bf16),
            dma((4,)),
            dma((8,)),
            dma(()),
            dma(()),
            dma((plane, CHUNKS)),
            dma((2, plane, CHUNKS)),
            dma((plane,)),
            dma((2, plane)),
            dma((2, CHUNKS)),
            dma((2, CHUNKS)),
            dma((2, plane, CHUNKS)),
            dma((plane, CHUNKS)),
        ],
        compiler_params=pltpu.CompilerParams(
            collective_id=1, has_side_effects=True, vmem_limit_bytes=VMEM_LIMIT
        ),
        name="triangle",
    )(pair, pair_mask, *columns, w_edges, w_gate, w_out)


def solution(mesh):
    sizes = dict(mesh.shape)
    depth = sizes["res"] // PLANE_ROWS
    body = wide_body
    if sizes["chan"] == 2 and sizes["res"] % PLANE_ROWS == 0 and depth == 4:
        body = functools.partial(plane_body, depth)
    return jax.shard_map(
        body,
        mesh=mesh,
        in_specs=(
            P(("groups", "chan"), "res", None),
            P(("groups", "res"), "chan"),
            P(),
            P(),
            P(),
            P(),
            P(),
            P(),
            P(),
        ),
        out_specs=P("groups", "res", "chan"),
        check_vma=False,
    )
```

```python
import functools

import jax
import jax.numpy as jnp
from jax import lax
from jax.experimental import pallas as pl
from jax.experimental.pallas import tpu as pltpu
from jax.sharding import PartitionSpec as P

epsilon = 1e-05
MESH = pl.DeviceIdType.MESH
PLANE_ROWS = 4
CHUNKS = 4
UNROLL = 16
VMEM_LIMIT = 52 * 1024 * 1024


def layer_norm(values, scale_gain, shift_bias):
    average = jnp.mean(values, axis=0, keepdims=True)
    centered = values - average
    variance = jnp.mean(centered * centered, axis=0, keepdims=True)
    return (
        centered * lax.rsqrt(variance + epsilon) * scale_gain[:, None, None]
        + shift_bias[:, None, None]
    )


def project_edges(normed, mask_block, w_edges):
    hidden = w_edges.shape[1] // 4
    maskf = mask_block.astype(jnp.float32)[None]

    def edge_half(offset):
        gate_part = jnp.einsum(
            "cij,ch->hij",
            normed,
            w_edges[:, offset : offset + hidden],
            preferred_element_type=jnp.float32,
        )
        value_part = jnp.einsum(
            "cij,ch->hij",
            normed,
            w_edges[:, offset + hidden : offset + 2 * hidden],
            preferred_element_type=jnp.float32,
        )
        return (jax.nn.sigmoid(gate_part) * value_part * maskf).astype(jnp.bfloat16)

    return (edge_half(0), edge_half(2 * hidden))


def finish(normed, product_normed, w_gate, w_out):
    gate_values = jax.nn.sigmoid(
        jnp.einsum("cij,cd->dij", normed, w_gate, preferred_element_type=jnp.float32)
    )
    mixed_out = jnp.einsum("hij,hd->dij", product_normed, w_out, preferred_element_type=jnp.float32)
    return (gate_values * mixed_out).astype(jnp.bfloat16)


def wide_body(pair, pair_mask, norm_gain, norm_bias, w_edges, w_gate, out_gain, out_bias, w_out):
    quarter = pair_mask.shape[1]
    whole_rows, mask_rows = (
        lax.all_gather(pair, "chan", axis=0, tiled=True),
        lax.all_gather(pair_mask, "chan", axis=1, tiled=True),
    )
    normed_rows = layer_norm(whole_rows.astype(jnp.float32), norm_gain, norm_bias).astype(
        jnp.bfloat16
    )
    left_edges, right_edges = project_edges(normed_rows, mask_rows, w_edges)
    left_edges, right_edges = (
        lax.all_to_all(left_edges, "res", split_axis=0, concat_axis=1, tiled=True),
        lax.all_to_all(right_edges, "res", split_axis=0, concat_axis=1, tiled=True),
    )
    right_slice = lax.dynamic_slice_in_dim(
        right_edges, lax.axis_index("chan") * quarter, quarter, 1
    )
    product = jnp.einsum(
        "cik,cjk->cij", left_edges, right_slice, preferred_element_type=jnp.float32
    )
    normed = lax.dynamic_slice_in_dim(normed_rows, lax.axis_index("chan") * quarter, quarter, 2)
    returned = lax.all_to_all(
        product.astype(jnp.bfloat16), "res", split_axis=1, concat_axis=0, tiled=True
    )
    product_normed = layer_norm(returned.astype(jnp.float32), out_gain, out_bias).astype(
        jnp.bfloat16
    )
    return finish(normed, product_normed, w_gate, w_out)


def centre(source):
    values = source.astype(jnp.float32)
    average = jnp.mean(values, axis=0, keepdims=True)
    centered = values - average
    variance = jnp.mean(centered * centered, axis=0, keepdims=True)
    return centered * lax.rsqrt(variance + epsilon)


def triangle_kernel(
    pair_ref,
    mask_ref,
    norm_gain_ref,
    norm_bias_ref,
    out_gain_ref,
    out_bias_ref,
    edges_ref,
    gate_ref,
    last_ref,
    out_ref,
    whole,
    mask,
    columns,
    edges,
    gate_weight,
    last_weight,
    edges_t,
    gate_t,
    last_t,
    wide,
    scaled,
    staged,
    normed,
    gates,
    left_ref,
    right_ref,
    lefts,
    rights,
    products,
    returned,
    local_sem,
    load_sem,
    pair_send,
    pair_recv,
    right_send,
    right_recv,
    left_send,
    left_recv,
    hop_send,
    hop_recv,
    back_send,
    back_recv,
):
    groups, res, x = lax.axis_index("groups"), lax.axis_index("res"), lax.axis_index("chan")
    z, r = res // PLANE_ROWS, res % PLANE_ROWS
    plane = 2 * PLANE_ROWS
    p = r * 2 + x
    rows, cols = left_ref.shape[1], left_ref.shape[2]
    half = pair_ref.shape[0]
    channels, hidden = normed.shape[1], left_ref.shape[0]
    mine = left_ref.shape[0] // plane
    step = mine // CHUNKS
    tall = PLANE_ROWS * rows

    loads = [
        pltpu.make_async_copy(source, target, load_sem.at[index])
        for index, (source, target) in enumerate(
            (
                (norm_gain_ref, columns.at[0]),
                (norm_bias_ref, columns.at[1]),
                (out_gain_ref, columns.at[2]),
                (out_bias_ref, columns.at[3]),
                (edges_ref, edges),
                (gate_ref, gate_weight),
                (last_ref, last_weight),
                (mask_ref, mask),
            )
        )
    ]
    place = whole.at[pl.ds(x * half, half)]
    own_pair = pltpu.make_async_copy(
        pair_ref.at[:, :, pl.ds(pl.multiple_of(x * cols, cols), cols)], place, local_sem.at[3]
    )
    own_pair.start()
    for load in loads:
        load.start()

    pod = z // 2
    hub_z, end_z = 1 + pod, 3 * pod
    is_hub = z == hub_z
    kind = jnp.where(is_hub, 0, 1)
    first = jnp.where(is_hub, 1, 0)

    def device(q, plane_z):
        return (groups, plane_z * PLANE_ROWS + q // 2, q % 2)

    def peer(offset):
        return (p + offset) % plane

    barrier = pltpu.get_barrier_semaphore()

    def signal(target):
        pl.semaphore_signal(barrier, inc=1, device_id=target, device_id_type=MESH)

    def greet(offset, carry):
        signal(device(peer(offset), hub_z))
        return carry

    def greet_end(offset, carry):
        signal(device(peer(offset), end_z))
        return carry

    lax.fori_loop(first, plane, greet, 0)

    @pl.when(is_hub)
    def _():
        lax.fori_loop(0, plane, greet_end, 0)
        signal(device(p, 3 - hub_z))

    @pl.when(z == end_z)
    def _():
        signal((groups, res, 1 - x))

    pl.semaphore_wait(barrier, jnp.where(is_hub, 2 * plane, plane + 1))

    other = 1 - x
    swap = pltpu.make_async_remote_copy(
        src_ref=pair_ref.at[:, :, pl.ds(pl.multiple_of(other * cols, cols), cols)],
        dst_ref=place,
        send_sem=pair_send,
        recv_sem=pair_recv,
        device_id=(groups, res, other),
        device_id_type=MESH,
    )
    swap.start()
    for load in loads:
        load.wait()
    for index in range(4):
        wide[index] = jnp.broadcast_to(columns[index], wide.shape[:0:-1]).T
    edges_t[...] = edges[...].T
    gate_t[...] = gate_weight[...].T
    last_t[...] = last_weight[...].T
    own_pair.wait()
    swap.wait_recv()
    scaled[...] = centre(whole[...]).reshape(scaled.shape)

    def line(i, count):
        return pl.ds(i, count, stride=rows)

    def project(i, offset):
        parts = jnp.dot(
            edges_t[offset : offset + 2 * hidden, :], normed[i], preferred_element_type=jnp.float32
        )
        valid = mask[pl.ds(i, 1), :].astype(jnp.float32)
        staged[line(i, hidden), :] = jax.nn.sigmoid(parts[:hidden]) * parts[hidden:] * valid

    def right_row(i, carry):
        values = scaled[line(i, channels), :] * wide[0] + wide[1]
        normed[i] = values.astype(normed.dtype)
        project(i, 2 * hidden)
        return carry

    def left_row(i, carry):
        project(i, 0)
        return carry

    def gate_row(i, carry):
        gates[i] = jax.nn.sigmoid(
            jnp.dot(gate_t[...], normed[i], preferred_element_type=jnp.float32)
        )
        return carry

    lax.fori_loop(0, rows, right_row, 0, unroll=UNROLL)
    right_ref[...] = staged[...].reshape(right_ref.shape).astype(right_ref.dtype)

    here = pl.ds(pl.multiple_of(z * tall + r * rows, rows), rows)
    here_left = pl.ds(pl.multiple_of(r * rows, rows), rows)
    here_cols = pl.ds(pl.multiple_of(x * cols, cols), cols)

    def right_copy(offset, c, sender):
        q = peer(offset)
        return pltpu.make_async_remote_copy(
            src_ref=right_ref.at[pl.ds(q * mine + c * step, step)],
            dst_ref=rights.at[pl.ds(c * step, step), here, here_cols],
            send_sem=right_send.at[offset, c],
            recv_sem=right_recv.at[sender, offset, c],
            device_id=device(q, hub_z),
            device_id_type=MESH,
        )

    def left_copy(offset, sender):
        q = peer(offset)
        return pltpu.make_async_remote_copy(
            src_ref=left_ref.at[pl.ds(q * mine, mine)],
            dst_ref=lefts.at[kind, :, here_left, here_cols],
            send_sem=left_send.at[offset],
            recv_sem=left_recv.at[sender, offset],
            device_id=device(q, hub_z),
            device_id_type=MESH,
        )

    own_right = pltpu.make_async_copy(
        right_ref.at[pl.ds(p * mine, mine)], rights.at[:, here, here_cols], local_sem.at[0]
    )
    own_left = pltpu.make_async_copy(
        left_ref.at[pl.ds(p * mine, mine)], lefts.at[0, :, here_left, here_cols], local_sem.at[1]
    )

    def over_peers(start, act):
        def one(offset, carry):
            act(offset)
            return carry

        lax.fori_loop(start, plane, one, 0)

    for c in range(CHUNKS):
        over_peers(first, lambda offset: right_copy(offset, c, kind).start())

    @pl.when(is_hub)
    def _():
        own_right.start()

    lax.fori_loop(0, rows, left_row, 0, unroll=UNROLL)
    left_ref[...] = staged[...].reshape(left_ref.shape).astype(left_ref.dtype)
    over_peers(first, lambda offset: left_copy(offset, kind).start())

    def hop(owner, c, sender):
        block = rights.at[
            pl.ds(c * step, step), pl.ds(pl.multiple_of(owner * tall, tall), tall), :
        ]
        return pltpu.make_async_remote_copy(
            src_ref=block,
            dst_ref=block,
            send_sem=hop_send.at[sender, c],
            recv_sem=hop_recv.at[sender, c],
            device_id=device(p, 3 - hub_z),
            device_id_type=MESH,
        )

    @pl.when(is_hub)
    def _():
        own_left.start()
        own_right.wait()
        for c in range(CHUNKS):
            over_peers(1, lambda offset: right_copy(offset, c, 0).wait_recv())
            hop(hub_z, c, 0).start()

    lax.fori_loop(0, rows, gate_row, 0, unroll=UNROLL)

    def back_copy(member, r_to, side, c):
        q = r_to * 2 + side
        offset = (q - p + plane) % plane
        return pltpu.make_async_remote_copy(
            src_ref=products.at[
                member,
                side,
                pl.ds(c * step, step),
                pl.ds(pl.multiple_of(r_to * rows, rows), rows),
                :,
            ],
            dst_ref=returned.at[pl.ds(p * mine + c * step, step)],
            send_sem=back_send.at[member, offset, c],
            recv_sem=back_recv.at[offset, c],
            device_id=device(q, end_z if member else hub_z),
            device_id_type=MESH,
        )

    def multiply(member, side, c):
        part = pl.ds(c * step, step)
        result = lax.dot_general(
            lefts[member, part],
            rights[part, pl.ds(pl.multiple_of(side * cols, cols), cols), :],
            (((2,), (2,)), ((0,), (0,))),
            preferred_element_type=jnp.float32,
        )
        products[member, side, part] = result.astype(products.dtype)

        def give(r_to, carry):
            if member:
                back_copy(member, r_to, side, c).start()
            else:

                @pl.when(r_to * 2 + side != p)
                def _():
                    back_copy(member, r_to, side, c).start()

            return carry

        lax.fori_loop(0, PLANE_ROWS, give, 0)

    own_back = pltpu.make_async_copy(
        products.at[0, x, :, here_left, :], returned.at[pl.ds(p * mine, mine)], local_sem.at[2]
    )

    @pl.when(is_hub)
    def _():
        for c in range(CHUNKS):
            over_peers(0, lambda offset: right_copy(offset, c, 1).wait_recv())
            hop(end_z, c, 1).start()
        own_left.wait()
        over_peers(1, lambda offset: left_copy(offset, 0).wait_recv())
        for c in range(CHUNKS):
            multiply(0, pod, c)
        over_peers(0, lambda offset: left_copy(offset, 1).wait_recv())
        for c in range(CHUNKS):
            multiply(1, pod, c)
        for c in range(CHUNKS):
            hop(3 - hub_z, c, 0).wait_recv()
            hop(3 - end_z, c, 1).wait_recv()
            multiply(1, 1 - pod, c)
            multiply(0, 1 - pod, c)
        own_back.start()
        own_back.wait()

    def back_of(member, offset, c):
        q = peer(offset)
        return back_copy(member, q // 2, q % 2, c)

    for c in range(CHUNKS):
        over_peers(first, lambda offset: back_of(0, offset, c).wait_recv())
    scaled[...] = centre(returned[...]).reshape(scaled.shape)

    def last_row(i, carry):
        values = scaled[line(i, hidden), :] * wide[2] + wide[3]
        mixed = jnp.dot(
            last_t[...], values.astype(jnp.bfloat16), preferred_element_type=jnp.float32
        )
        staged[line(i, channels), :] = gates[i] * mixed
        return carry

    lax.fori_loop(0, rows, last_row, 0, unroll=UNROLL)
    out_ref[...] = staged[...].reshape(out_ref.shape).astype(out_ref.dtype)

    for c in range(CHUNKS):
        over_peers(first, lambda offset: right_copy(offset, c, kind).wait_send())

        @pl.when(is_hub)
        def _():
            over_peers(1, lambda offset: back_of(0, offset, c).wait_send())
            over_peers(0, lambda offset: back_of(1, offset, c).wait_send())
            hop(hub_z, c, 0).wait_send()
            hop(end_z, c, 1).wait_send()

    over_peers(first, lambda offset: left_copy(offset, kind).wait_send())
    swap.wait_send()


def plane_body(
    depth, pair, pair_mask, norm_gain, norm_bias, w_edges, w_gate, out_gain, out_bias, w_out
):
    rows, cols = pair_mask.shape
    channels, hidden = w_gate.shape[0], w_out.shape[0]
    width = 2 * cols
    plane = 2 * PLANE_ROWS
    mine = hidden // plane
    tall = PLANE_ROWS * rows
    dma = pltpu.SemaphoreType.DMA

    columns = [v[None] for v in (norm_gain, norm_bias, out_gain, out_bias)]
    operands = [
        pltpu.with_memory_space_constraint(operand, pltpu.HBM)
        for operand in (pair, pair_mask, *columns, w_edges, w_gate, w_out)
    ]
    bf16, f32 = jnp.bfloat16, jnp.float32
    return pl.pallas_call(
        triangle_kernel,
        out_shape=jax.ShapeDtypeStruct((channels, rows, cols), bf16),
        in_specs=[pl.BlockSpec(memory_space=pltpu.HBM)] * 9,
        out_specs=pl.BlockSpec(memory_space=pltpu.VMEM),
        scratch_shapes=[
            pltpu.VMEM((channels, rows, cols), bf16),
            pltpu.VMEM(pair_mask.shape, pair_mask.dtype),
            pltpu.VMEM((4, 1, channels), f32),
            pltpu.VMEM(w_edges.shape, bf16),
            pltpu.VMEM(w_gate.shape, bf16),
            pltpu.VMEM(w_out.shape, bf16),
            pltpu.VMEM(w_edges.shape[::-1], bf16),
            pltpu.VMEM(w_gate.shape[::-1], bf16),
            pltpu.VMEM(w_out.shape[::-1], bf16),
            pltpu.VMEM((4, channels, cols), f32),
            pltpu.VMEM((channels * rows, cols), f32),
            pltpu.VMEM((hidden * rows, cols), f32),
            pltpu.VMEM((rows, channels, cols), bf16),
            pltpu.VMEM((rows, channels, cols), f32),
            pltpu.VMEM((hidden, rows, cols), bf16),
            pltpu.VMEM((hidden, rows, cols), bf16),
            pltpu.VMEM((2, mine, tall, width), bf16),
            pltpu.VMEM((mine, depth * tall, width), bf16),
            pltpu.VMEM((2, 2, mine, tall, cols), bf16),
            pltpu.VMEM((hidden, rows, cols), bf16),
            dma((4,)),
            dma((8,)),
            dma(()),
            dma(()),
            dma((plane, CHUNKS)),
            dma((2, plane, CHUNKS)),
            dma((plane,)),
            dma((2, plane)),
            dma((2, CHUNKS)),
            dma((2, CHUNKS)),
            dma((2, plane, CHUNKS)),
            dma((plane, CHUNKS)),
        ],
        compiler_params=pltpu.CompilerParams(
            collective_id=1, has_side_effects=True, vmem_limit_bytes=VMEM_LIMIT
        ),
        name="triangle",
    )(*operands)


def solution(mesh):
    sizes = dict(mesh.shape)
    depth = sizes["res"] // PLANE_ROWS
    body = wide_body
    if sizes["chan"] == 2 and sizes["res"] % PLANE_ROWS == 0 and depth == 4:
        body = functools.partial(plane_body, depth)
    return jax.shard_map(
        body,
        mesh=mesh,
        in_specs=(
            P(("groups", "chan"), "res", None),
            P(("groups", "res"), "chan"),
            P(),
            P(),
            P(),
            P(),
            P(),
            P(),
            P(),
        ),
        out_specs=P("groups", "res", "chan"),
        check_vma=False,
    )
```
